256 devices in a mesh: dom: 32 (over y, x, core), slab: 8 (over z).
Axes of the slice: x: 4, y: 4, z: 8, core: 2. Of those that a mesh axis runs over, the one named last changes fastest.
Arguments:
- nullspace: float32 [6, 1179648], P(None, ('dom', 'slab')), may hold values from -6 to 6
- owner_device: int32 [1179648], P(('dom', 'slab')), may hold values from 0 to 255, as said below
- local_aggregate: int32 [1179648], P(('dom', 'slab')), may hold values from 0 to 63, as said below
- position: int32 [1179648], P(('dom', 'slab')), may hold values from 0 to 127, as said below
- sent_rows: int32 [256, 256, 18], P(('dom', 'slab')), may hold values from -1 to 4607, as said below
- arrival_slot: int32 [256, 256, 18], P(('dom', 'slab')), may hold values from -1 to 8191, as said below
Outputs:
- prolongator: float32 [6, 1179648], P(None, ('dom', 'slab'))
- padded_prolongator: float32 [6, 2097152], P(None, ('dom', 'slab'))
- coarse_nullspace: float32 [36, 16384], P(None, ('dom', 'slab'))
The draws below stay inside these ranges and needn't reach their ends.
Inputs may be any that keep to these rules, and one draw needn't show every extreme that they name: `owner_device`: devices are numbered in dom+slab order. A device holds 4608 rows and owns 64 aggregates; the aggregates of one owner hold 4608 rows in all, each 16 to 128 rows, a multiple of 8, and every owner has an aggregate of 128 rows. The aggregate's global number is owner_device * 64 + local_aggregate. `position`: distinct among the rows of one aggregate and below that aggregate's row count. `sent_rows`: entry [p, q, k] is the k-th row of device p (a local row index) whose aggregate device q owns; every row of p owned elsewhere stands exactly once, live entries of [p, q] come first and -1 fills the rest; [p, p] is empty; [p, q] and [q, p] have equally many live entries, at most 18, and some pair has 18. `arrival_slot`: entry [q, p, k] is local_aggregate * 128 + position of the row sent_rows[p, q, k], -1 where that is -1.
All inputs are finite; a program needn't handle non-finite values.
Results may differ from the reference program's by a relative error of at most 0.0003.
Values sent between devices are 32-bit elements; how exact they have to be, the bound alone decides.
No kernel may reach another device: no remote copies, remote signals or barrier semaphores. Data moves between devices by JAX's collectives and lax.ppermute only.
A program may use at most 64 MiB of HBM per device.

```python
import jax
import jax.numpy as jnp
from jax import lax

MODES = 6
PAD = 128
AGG_DEV = 64
ROWS_DEV = 4608
CAP = 18
ROWS = 1179648
DEVICES = 256


def plan_tables(key):
    subkeys = jax.random.split(key, 8)
    half_count = AGG_DEV // 2
    steps_k = jax.random.randint(subkeys[0], (DEVICES, half_count), -7, 8)
    chosen_pair = jax.random.randint(subkeys[1], (DEVICES, 1), 0, half_count)
    steps_k = jnp.where(jnp.arange(half_count)[None, :] == chosen_pair, 7, steps_k)
    agg_sizes = jnp.stack([72 + 8 * steps_k, 72 - 8 * steps_k], axis=2).reshape(DEVICES, AGG_DEV).astype(jnp.int32)
    agg_ends = jnp.cumsum(agg_sizes, axis=1).astype(jnp.int32)
    starts = agg_ends - agg_sizes
    slot_ids = jnp.arange(ROWS_DEV, dtype=jnp.int32)
    slot_agg = jax.vmap(lambda edges_row: jnp.searchsorted(edges_row, slot_ids, side='right'))(agg_ends).astype(jnp.int32)
    slot_place = slot_agg * PAD + slot_ids[None, :] - jnp.take_along_axis(starts, slot_agg, axis=1)
    first_draw = jax.random.randint(subkeys[2], (DEVICES, DEVICES), 0, CAP + 1)
    second_draw = jax.random.randint(subkeys[3], (DEVICES, DEVICES), 0, CAP + 1)
    upper_part = jnp.triu(jnp.maximum(first_draw, second_draw), 1)
    pair_count = (upper_part + upper_part.T).astype(jnp.int32)
    pick_first = jax.random.randint(subkeys[4], (), 0, DEVICES)
    pick_second = (pick_first + jax.random.randint(subkeys[5], (), 1, DEVICES)) % DEVICES
    pair_count = pair_count.at[pick_first, pick_second].set(CAP).at[pick_second, pick_first].set(CAP)
    offsets = (jnp.cumsum(pair_count, axis=1) - pair_count).astype(jnp.int32)
    inclusive = jnp.cumsum(pair_count, axis=1).astype(jnp.int32)
    lent_total = jnp.sum(pair_count, axis=1).astype(jnp.int32)
    kept_count = ROWS_DEV - lent_total
    slot_order = jax.vmap(lambda subkey: jax.random.permutation(subkey, ROWS_DEV))(jax.random.split(subkeys[6], DEVICES)).astype(jnp.int32)
    row_order = jax.vmap(lambda subkey: jax.random.permutation(subkey, ROWS_DEV))(jax.random.split(subkeys[7], DEVICES)).astype(jnp.int32)
    borrowed = slot_ids[None, :] - kept_count[:, None]
    lender = jax.vmap(lambda cum_row, ask_row: jnp.searchsorted(cum_row, ask_row, side='right'))(inclusive, jnp.maximum(borrowed, 0)).astype(jnp.int32)
    lender = jnp.minimum(lender, DEVICES - 1)
    device_ids = jnp.arange(DEVICES, dtype=jnp.int32)[:, None]
    within_lent = borrowed - jnp.take_along_axis(offsets, lender, axis=1)
    from_lender = slot_order[lender, jnp.clip(offsets[lender, device_ids] + within_lent, 0, ROWS_DEV - 1)]
    own_slot = jnp.take_along_axis(slot_order, jnp.clip(lent_total[:, None] + slot_ids[None, :], 0, ROWS_DEV - 1), axis=1)
    is_kept = borrowed < 0
    entry_owner = jnp.where(is_kept, device_ids, lender)
    entry_slot = jnp.where(is_kept, own_slot, from_lender)
    entry_place = slot_place[entry_owner, entry_slot]
    owner_rows = jnp.take_along_axis(entry_owner, row_order, axis=1)
    place_rows = jnp.take_along_axis(entry_place, row_order, axis=1)
    inverse_order = jnp.argsort(row_order, axis=1).astype(jnp.int32)
    lane_ids = jnp.arange(CAP, dtype=jnp.int32)[None, None, :]
    live_slot = lane_ids < pair_count[:, :, None]
    entry_sent = kept_count[:, None, None] + offsets[:, :, None] + lane_ids
    sent_table = jnp.take_along_axis(inverse_order, jnp.clip(entry_sent, 0, ROWS_DEV - 1).reshape(DEVICES, -1), axis=1)
    sent_table = jnp.where(live_slot, sent_table.reshape(DEVICES, DEVICES, CAP), -1)
    lent_slot = jnp.take_along_axis(slot_order, jnp.clip(offsets[:, :, None] + lane_ids, 0, ROWS_DEV - 1).reshape(DEVICES, -1), axis=1)
    arrival = jnp.take_along_axis(slot_place, lent_slot, axis=1).reshape(DEVICES, DEVICES, CAP)
    arrival = jnp.where(live_slot, arrival, -1)
    return (owner_rows.reshape(-1).astype(jnp.int32), (place_rows // PAD).reshape(-1).astype(jnp.int32), (place_rows % PAD).reshape(-1).astype(jnp.int32), sent_table.astype(jnp.int32), arrival.astype(jnp.int32))


def draw_owner_device(key, part):
    return plan_tables(jax.random.fold_in(key, 11))[0]


def draw_local_aggregate(key, part):
    return plan_tables(jax.random.fold_in(key, 11))[1]


def draw_position(key, part):
    return plan_tables(jax.random.fold_in(key, 11))[2]


def draw_sent_rows(key, part):
    return plan_tables(jax.random.fold_in(key, 11))[3]


def draw_arrival_slot(key, part):
    return plan_tables(jax.random.fold_in(key, 11))[4]


def shard_levels(stream_key, dims, shards, low, largest):
    def one(axis_at, parts):
        heights = jax.random.uniform(jax.random.fold_in(jax.random.fold_in(stream_key, 6), axis_at), (parts,), jnp.float32, low / len(shards), largest / len(shards))
        return jnp.repeat(jnp.exp(heights), dims[axis_at] // parts).reshape((-1,) + (1,) * (len(dims) - axis_at - 1))

    loudness = one(*shards[0])
    for cut in shards[1:]:
        loudness = loudness * one(*cut)
    return loudness


def scatter_about(own_key, extent, deviation, most, cuts=(), kind=jnp.bfloat16):
    values = deviation * jax.random.normal(own_key, extent, jnp.float32)
    if cuts:
        values = values * shard_levels(own_key, extent, cuts, -0.22, 0.18)
    return jnp.clip(values, -most, most).astype(kind)


def setup_inputs(seed: int = 0) -> dict:
    keys = jax.random.split(jax.random.key(seed), 7)
    nullspace = scatter_about(keys[0], (MODES, ROWS), 1.0, 6.0, ((1, 256),), jnp.float32)
    owner_device = draw_owner_device(jax.random.fold_in(keys[6], 71), 0)
    local_aggregate = draw_local_aggregate(jax.random.fold_in(keys[6], 71), 0)
    position = draw_position(jax.random.fold_in(keys[6], 71), 0)
    sent_rows = draw_sent_rows(jax.random.fold_in(keys[6], 71), 0)
    arrival_slot = draw_arrival_slot(jax.random.fold_in(keys[6], 71), 0)
    return dict(nullspace=nullspace, owner_device=owner_device, local_aggregate=local_aggregate, position=position, sent_rows=sent_rows, arrival_slot=arrival_slot)


def cholesky_upper(gram_terms, mode_count):
    factor_up = [[jnp.zeros_like(gram_terms[0][0]) for right_j in range(mode_count)] for left_i in range(mode_count)]
    for left_i in range(mode_count):
        pivot_sq = gram_terms[left_i][left_i]
        for inner_k in range(left_i):
            pivot_sq = pivot_sq - factor_up[inner_k][left_i] * factor_up[inner_k][left_i]
        pivot_val = jnp.sqrt(pivot_sq)
        factor_up[left_i][left_i] = pivot_val
        for right_j in range(left_i + 1, mode_count):
            partial_ij = gram_terms[left_i][right_j]
            for inner_k in range(left_i):
                partial_ij = partial_ij - factor_up[inner_k][left_i] * factor_up[inner_k][right_j]
            factor_up[left_i][right_j] = partial_ij / pivot_val
    return factor_up

def invert_upper(factor_up, mode_count):
    inverse = [[jnp.zeros_like(factor_up[0][0]) for right_j in range(mode_count)] for left_i in range(mode_count)]
    for left_i in range(mode_count):
        inverse[left_i][left_i] = 1.0 / factor_up[left_i][left_i]
        for right_j in range(left_i + 1, mode_count):
            partial_ij = jnp.zeros_like(factor_up[0][0])
            for inner_k in range(left_i, right_j):
                partial_ij = partial_ij + inverse[left_i][inner_k] * factor_up[inner_k][right_j]
            inverse[left_i][right_j] = -partial_ij / factor_up[right_j][right_j]
    return inverse

def apply_inverse(columns, inverse, mode_count):
    results = []
    for right_j in range(mode_count):
        total_j = columns[0] * inverse[0][right_j]
        for left_i in range(1, right_j + 1):
            total_j = total_j + columns[left_i] * inverse[left_i][right_j]
        results.append(total_j)
    return jnp.stack(results)

def gram_of(padded_rows):
    mode_count = padded_rows.shape[0]
    shaped = padded_rows.reshape(mode_count, AGG_DEV, PAD)
    return jnp.einsum('iap,kap->ika', shaped, shaped, precision=lax.Precision.HIGHEST)

def factor_block(padded_rows, gram_sum):
    mode_count = padded_rows.shape[0]
    shaped = padded_rows.reshape(mode_count, AGG_DEV, PAD)
    gram_terms = [[gram_sum[left_i, right_j] for right_j in range(mode_count)] for left_i in range(mode_count)]
    factor_up = cholesky_upper(gram_terms, mode_count)
    inverse = invert_upper(factor_up, mode_count)
    widened = [[entry_value[:, None] for entry_value in inverse_row] for inverse_row in inverse]
    padded_q = apply_inverse([shaped[left_i] for left_i in range(mode_count)], widened, mode_count)
    padded_q = padded_q.reshape(mode_count, -1)
    coarse = jnp.stack([factor_up[left_i][right_j] for left_i in range(mode_count) for right_j in range(mode_count)])
    inverse_table = jnp.stack([inverse[left_i][right_j] for left_i in range(mode_count) for right_j in range(left_i, mode_count)])
    return (padded_q, coarse, inverse_table)

def fine_values(columns, chosen):
    mode_count = columns.shape[0]
    inverse = [[jnp.zeros_like(columns[0]) for right_j in range(mode_count)] for left_i in range(mode_count)]
    counter = 0
    for left_i in range(mode_count):
        for right_j in range(left_i, mode_count):
            inverse[left_i][right_j] = chosen[counter]
            counter = counter + 1
    return apply_inverse([columns[left_i] for left_i in range(mode_count)], inverse, mode_count)

def reference(nullspace, owner_device, local_aggregate, position, sent_rows, arrival_slot):
    mode_count = nullspace.shape[0]
    slot_count = AGG_DEV * PAD
    block_base = (jnp.arange(DEVICES, dtype=jnp.int32) * ROWS_DEV)[:, None]

    def per_owner(owner_q):
        start_row = owner_q * ROWS_DEV
        own_rows = lax.dynamic_slice_in_dim(nullspace, start_row, ROWS_DEV, 1)
        own_owner = lax.dynamic_slice_in_dim(owner_device, start_row, ROWS_DEV, 0)
        own_agg = lax.dynamic_slice_in_dim(local_aggregate, start_row, ROWS_DEV, 0)
        own_pos = lax.dynamic_slice_in_dim(position, start_row, ROWS_DEV, 0)
        local_slot = jnp.where(own_owner == owner_q, own_agg * PAD + own_pos, slot_count)
        senders = sent_rows[:, owner_q, :]
        live_in = senders >= 0
        global_rows = jnp.where(live_in, senders + block_base, 0).reshape(-1)
        arrived = jnp.take(nullspace, global_rows, axis=1)
        landing = arrival_slot[owner_q].reshape(-1)
        landing_safe = jnp.where(landing >= 0, landing, slot_count)
        padded_rows = jnp.zeros((mode_count, slot_count), jnp.float32)
        padded_rows = padded_rows.at[:, local_slot].set(own_rows, mode='drop')
        padded_rows = padded_rows.at[:, landing_safe].set(arrived, mode='drop')
        return factor_block(padded_rows, gram_of(padded_rows))
    device_list = jnp.arange(DEVICES, dtype=jnp.int32)
    padded_all, coarse_all, table_all = lax.map(per_owner, device_list)
    padded_out = jnp.transpose(padded_all, (1, 0, 2)).reshape(mode_count, -1)
    coarse_out = jnp.transpose(coarse_all, (1, 0, 2)).reshape(mode_count * mode_count, -1)
    whole_table = jnp.transpose(table_all, (1, 0, 2)).reshape(table_all.shape[1], -1)

    def per_block(block_q):
        start_row = block_q * ROWS_DEV
        rows_here = lax.dynamic_slice_in_dim(nullspace, start_row, ROWS_DEV, 1)
        owners_here = lax.dynamic_slice_in_dim(owner_device, start_row, ROWS_DEV, 0)
        aggs_here = lax.dynamic_slice_in_dim(local_aggregate, start_row, ROWS_DEV, 0)
        global_ids = owners_here * AGG_DEV + aggs_here
        return fine_values(rows_here, jnp.take(whole_table, global_ids, axis=1))
    fine_all = lax.map(per_block, device_list)
    fine_out = jnp.transpose(fine_all, (1, 0, 2)).reshape(mode_count, -1)
    return (fine_out, padded_out, coarse_out)
```

```python
import jax
import jax.numpy as jnp
from jax import lax
from jax.experimental import pallas as pl
from jax.experimental.pallas import tpu as pltpu
from jax.sharding import PartitionSpec as P

PAD = 128
AGG_DEV = 64
MODES = 6
ROWS = 4608
CHUNKS = 36
LANES = 18
PEERS = 256
GROUPS = (0, 8, 16, 24, 28)
AXES = ("dom", "slab")


def lane_take(table_row, lane_index):
    wide = jnp.broadcast_to(table_row, lane_index.shape)
    return jnp.take_along_axis(wide, lane_index, axis=1, mode="promise_in_bounds")


def row_iota(shape, dtype=jnp.int32):
    return lax.broadcasted_iota(jnp.int32, shape, 0).astype(dtype)


def one_hot_rows(values_row, iota_rows, scaled=None):
    hit = iota_rows == values_row
    payload = jnp.ones_like(iota_rows) if scaled is None else scaled
    return jnp.where(hit, payload, jnp.zeros_like(iota_rows))


def nt_dot(left, right):
    return lax.dot_general(left, right, (((1,), (1,)), ((), ())), preferred_element_type=jnp.float32)


def pick_kernel(rows_ref, sent_ref, send_ref, gathered_ref, message_ref):
    index = [jnp.maximum(sent_ref[g : g + 8, :], 0) for g in GROUPS]
    lane = [v & 127 for v in index]
    tile = [v >> 7 for v in index]
    for half in (slice(0, 3), slice(3, 6)):
        modes = range(MODES)[half]
        acc = {(m, g): jnp.zeros((8, 128), jnp.float32) for m in modes for g in range(5)}
        for t in range(CHUNKS):
            hits = [v == t for v in tile]
            for m in modes:
                row = rows_ref[m : m + 1, t * 128 : (t + 1) * 128]
                for g in range(5):
                    acc[m, g] = jnp.where(hits[g], lane_take(row, lane[g]), acc[m, g])
        for m in modes:
            for g in range(5):
                gathered_ref[m, GROUPS[g] : GROUPS[g] + 8, :] = acc[m, g]
    for h in range(2):
        message_ref[...] = jnp.zeros((128, 128), jnp.float32)
        for m in range(MODES):
            message_ref[pl.ds(m, LANES, stride=MODES), :] = gathered_ref[m, pl.ds(h, LANES, stride=2), :]
        send_ref[h * 128 : (h + 1) * 128, :] = message_ref[...].T


def split3(value):
    top = value.astype(jnp.bfloat16)
    rest = value - top.astype(jnp.float32)
    mid = rest.astype(jnp.bfloat16)
    low = (rest - mid.astype(jnp.float32)).astype(jnp.bfloat16)
    return top, mid, low


def gram_part(rows_of, aggregate_ref, left_ref, right_ref):
    agg_iota = row_iota((AGG_DEV, 128), jnp.bfloat16)
    for c in range(CHUNKS):
        cols = slice(c * 128, (c + 1) * 128)
        x = rows_of(c)
        for i in range(0, MODES, 2):
            pieces = split3(jnp.concatenate([x * x[i : i + 1, :], x * x[i + 1 : i + 2, :]], axis=0))
            for s in range(3):
                left_ref[s * 48 + i * 8 : s * 48 + i * 8 + 16, cols] = pieces[s]
        agg = aggregate_ref[c : c + 1, :].astype(jnp.float32).astype(jnp.bfloat16)
        right_ref[:, cols] = one_hot_rows(agg, agg_iota)
    full = nt_dot(left_ref[...], right_ref[...])
    return full[0:48] + (full[48:96] + full[96:144])


def own_kernel(me_ref, rows_ref, owner_ref, local_ref, place_ref, sent_ref, arrive_ref,
               gram_ref, fine_source_ref, slot_source_ref,
               rows8_ref, agg_ref, left_ref, right_ref, fl_ref, fr_ref, sl_ref, sr_ref):
    me = me_ref[0]
    owned = owner_ref[...] == me
    agg_ref[...] = jnp.where(owned, local_ref[...], -1)
    rows8_ref[0:MODES, :] = rows_ref[...]
    rows8_ref[MODES:8, :] = jnp.zeros((2, ROWS), jnp.float32)
    gram_ref[...] = gram_part(lambda c: rows8_ref[:, c * 128 : (c + 1) * 128], agg_ref, left_ref, right_ref)
    lane_row = lax.broadcasted_iota(jnp.int32, (1, 128), 1).astype(jnp.float32).astype(jnp.bfloat16)
    low_iota = row_iota((128, 128)).astype(jnp.float32).astype(jnp.bfloat16)
    hi48 = row_iota((48, 128)).astype(jnp.float32).astype(jnp.bfloat16)
    hi64 = row_iota((64, 128)).astype(jnp.float32).astype(jnp.bfloat16)
    lanes48 = jnp.broadcast_to(lane_row, (48, 128))
    lanes64 = jnp.broadcast_to(lane_row, (64, 128))

    def as_row(value):
        return value.astype(jnp.float32).astype(jnp.bfloat16)

    def part(c, hi_row, lo_row, hi_iota, lanes, left, right, number):
        cols = slice(c * 128, (c + 1) * 128)
        count = hi_iota.shape[0]
        left[0:count, cols] = one_hot_rows(hi_row, hi_iota, jnp.full_like(hi_iota, number))
        left[count : 2 * count, cols] = one_hot_rows(hi_row, hi_iota, lanes)
        right[:, cols] = one_hot_rows(lo_row, low_iota)

    for c in range(CHUNKS):
        sent = sent_ref[c : c + 1, :]
        part(c, as_row(sent >> 7), as_row(sent & 127), hi48, lanes48, fl_ref, fr_ref, c)
        part(c, as_row(agg_ref[c : c + 1, :]), as_row(place_ref[c : c + 1, :]), hi64, lanes64, sl_ref, sr_ref, c + 1)
        landing = arrive_ref[c : c + 1, :]
        part(CHUNKS + c, as_row(landing >> 7), as_row(landing & 127), hi64, lanes64, sl_ref, sr_ref, CHUNKS + c + 1)
    found = nt_dot(fl_ref[...], fr_ref[...])
    code = (found[0:48] * 128.0 + found[48:96]).astype(jnp.int32)
    fine_source_ref[...] = jnp.where(owned, -1, code[0:CHUNKS])
    found = nt_dot(sl_ref[...], sr_ref[...])
    slot_source_ref[...] = (found[0:64] * 128.0 + found[64:128]).astype(jnp.int32) - 128


def apply_tables(x, agg_row, table_ref):
    index = jnp.broadcast_to(agg_row, (8, 128))
    total = None
    for i in range(MODES):
        entry = jnp.take_along_axis(table_ref[i * 8 : (i + 1) * 8, :], index, axis=1, mode="promise_in_bounds")
        term = jnp.broadcast_to(x[i : i + 1, :], (8, 128)) * entry
        total = term if total is None else total + term
    return total


def factor_kernel(recv_ref, arrive_ref, gram_ref, send_ref, coarse_ref, table_ref, answer_ref,
                  rows8_ref, agg_ref, left_ref, right_ref, message_ref):
    landing = arrive_ref[...]
    agg_ref[...] = jnp.where(landing >= 0, landing >> 7, -1)
    rows8_ref[MODES:8, :] = jnp.zeros((2, ROWS), jnp.float32)
    for h in range(2):
        message_ref[...] = recv_ref[h * 128 : (h + 1) * 128, :].T
        for k in range(LANES):
            c = 2 * k + h
            rows8_ref[0:MODES, c * 128 : (c + 1) * 128] = message_ref[MODES * k : MODES * (k + 1), :]
    gram = gram_ref[...] + gram_part(lambda c: rows8_ref[:, c * 128 : (c + 1) * 128], agg_ref, left_ref, right_ref)
    g = [[gram[i * 8 + j : i * 8 + j + 1, :] for j in range(MODES)] for i in range(MODES)]
    up = [[None] * MODES for _ in range(MODES)]
    over = [None] * MODES
    zero = jnp.zeros((1, AGG_DEV), jnp.float32)
    for i in range(MODES):
        square = g[i][i]
        for k in range(i):
            square = square - up[k][i] * up[k][i]
        pivot = jnp.sqrt(square)
        up[i][i] = pivot
        over[i] = 1.0 / pivot
        for j in range(i + 1, MODES):
            rest = g[i][j]
            for k in range(i):
                rest = rest - up[k][i] * up[k][j]
            up[i][j] = rest * over[i]
    inv = [[None] * MODES for _ in range(MODES)]
    for i in range(MODES):
        inv[i][i] = over[i]
        for j in range(i + 1, MODES):
            total = inv[i][i] * up[i][j]
            for k in range(i + 1, j):
                total = total + inv[i][k] * up[k][j]
            inv[i][j] = -total * over[j]
    table_ref[...] = jnp.zeros((48, 128), jnp.float32)
    for i in range(MODES):
        for j in range(MODES):
            coarse_ref[i * MODES + j : i * MODES + j + 1, :] = up[i][j] if j >= i else zero
            if j >= i:
                table_ref[i * 8 + j : i * 8 + j + 1, 0:AGG_DEV] = inv[i][j]
    for h in range(2):
        message_ref[...] = jnp.zeros((128, 128), jnp.float32)
        for k in range(LANES):
            c = 2 * k + h
            cols = slice(c * 128, (c + 1) * 128)
            index = jnp.maximum(agg_ref[c : c + 1, :], 0)
            answer = apply_tables(rows8_ref[:, cols], index, table_ref)
            answer_ref[:, cols] = answer
            message_ref[MODES * k : MODES * (k + 1), :] = answer[0:MODES]
        send_ref[h * 128 : (h + 1) * 128, :] = message_ref[...].T


def padded_kernel(rows_ref, local_ref, table_ref, answer_ref, source_ref, padded_ref, own_ref, placed_ref):
    for c in range(CHUNKS):
        cols = slice(c * 128, (c + 1) * 128)
        own_ref[:, cols] = apply_tables(rows_ref[:, cols], local_ref[c : c + 1, :], table_ref)
    code = [source_ref[g * 8 : (g + 1) * 8, :] for g in range(8)]
    lane = [v & 127 for v in code]
    tile = [v >> 7 for v in code]
    for half in range(3):
        modes = range(2 * half, 2 * half + 2)
        acc = {(m, g): jnp.zeros((8, 128), jnp.float32) for m in modes for g in range(8)}
        for t in range(2 * CHUNKS):
            hits = [v == t for v in tile]
            part = own_ref if t < CHUNKS else answer_ref
            at = (t % CHUNKS) * 128
            for m in modes:
                row = part[m : m + 1, at : at + 128]
                for g in range(8):
                    acc[m, g] = jnp.where(hits[g], lane_take(row, lane[g]), acc[m, g])
        for m in modes:
            for g in range(8):
                placed_ref[m * 64 + g * 8 : m * 64 + g * 8 + 8, :] = acc[m, g]
    for a in range(AGG_DEV):
        padded_ref[:, a * 128 : (a + 1) * 128] = placed_ref[pl.ds(a, MODES, stride=AGG_DEV), :]


def fine_kernel(recv_ref, source_ref, own_ref, fine_ref, message_ref, placed_ref):
    for h in range(2):
        message_ref[h * 128 : (h + 1) * 128, :] = recv_ref[h * 128 : (h + 1) * 128, :].T
    code = [source_ref[g : g + 8, :] for g in GROUPS]
    lane = [v & 127 for v in code]
    tile = [v >> 7 for v in code]
    for half in (slice(0, 3), slice(3, 6)):
        modes = range(MODES)[half]
        acc = {(m, g): jnp.zeros((8, 128), jnp.float32) for m in modes for g in range(5)}
        for t in range(CHUNKS):
            hits = [v == t for v in tile]
            for m in modes:
                at = (t % 2) * 128 + MODES * (t // 2) + m
                row = message_ref[at : at + 1, :]
                for g in range(5):
                    acc[m, g] = jnp.where(hits[g], lane_take(row, lane[g]), acc[m, g])
        for m in modes:
            for g in range(5):
                placed_ref[m * 40 + GROUPS[g] : m * 40 + GROUPS[g] + 8, :] = acc[m, g]
    for c in range(CHUNKS):
        cols = slice(c * 128, (c + 1) * 128)
        away = jnp.broadcast_to(source_ref[c : c + 1, :] >= 0, (MODES, 128))
        fine_ref[:, cols] = jnp.where(away, placed_ref[pl.ds(c, MODES, stride=40), :], own_ref[0:MODES, cols])


def f32(*shape):
    return jax.ShapeDtypeStruct(shape, jnp.float32)


def i32(*shape):
    return jax.ShapeDtypeStruct(shape, jnp.int32)


def vm(*shape):
    return pltpu.VMEM(shape, jnp.float32)


def vb(*shape):
    return pltpu.VMEM(shape, jnp.bfloat16)


def call(kernel, out_shape, scratch, *args, scalar=False):
    specs = [pl.BlockSpec(memory_space=pltpu.VMEM) for _ in args]
    if scalar:
        specs[0] = pl.BlockSpec(memory_space=pltpu.SMEM)
    many = isinstance(out_shape, tuple)
    one = pl.BlockSpec(memory_space=pltpu.VMEM)
    return pl.pallas_call(
        kernel,
        out_shape=out_shape,
        in_specs=specs,
        out_specs=tuple(one for _ in out_shape) if many else one,
        scratch_shapes=scratch,
        compiler_params=pltpu.CompilerParams(vmem_limit_bytes=40 * 1024 * 1024),
        name=kernel.__name__,
    )(*args)


def exchange(message):
    return lax.all_to_all(message, AXES, 0, 0, tiled=True)


def body(nullspace, owner_device, local_aggregate, position, sent_rows, arrival_slot):
    me = (lax.axis_index("dom") * lax.axis_size("slab") + lax.axis_index("slab")).reshape(1)
    owner = owner_device.reshape(CHUNKS, 128)
    local = local_aggregate.reshape(CHUNKS, 128)
    place = position.reshape(CHUNKS, 128)
    sent = jnp.transpose(sent_rows[0], (1, 0)).reshape(CHUNKS, 128)
    arrive = jnp.transpose(arrival_slot[0], (1, 0)).reshape(CHUNKS, 128)
    send = call(pick_kernel, f32(PEERS, 128), [vm(MODES, 40, 128), vm(128, 128)], nullspace, sent)
    recv = exchange(send)
    gram_scratch = [vm(8, ROWS), pltpu.VMEM((CHUNKS, 128), jnp.int32), vb(144, ROWS), vb(AGG_DEV, ROWS)]
    gram, fine_source, slot_source = call(
        own_kernel,
        (f32(48, AGG_DEV), i32(CHUNKS, 128), i32(AGG_DEV, 128)),
        gram_scratch + [vb(96, ROWS), vb(128, ROWS), vb(128, 2 * ROWS), vb(128, 2 * ROWS)],
        me, nullspace, owner, local, place, sent, arrive,
        scalar=True,
    )
    send, coarse, table, answer = call(
        factor_kernel,
        (f32(PEERS, 128), f32(36, AGG_DEV), f32(48, 128), f32(8, ROWS)),
        gram_scratch + [vm(128, 128)],
        recv, arrive, gram,
    )
    recv = exchange(send)
    padded, own = call(
        padded_kernel,
        (f32(MODES, AGG_DEV * PAD), f32(8, ROWS)),
        [vm(MODES * AGG_DEV, 128)],
        nullspace, local, table, answer, slot_source,
    )
    fine = call(
        fine_kernel,
        f32(MODES, ROWS),
        [vm(256, 128), vm(MODES * 40, 128)],
        recv, fine_source, own,
    )
    return fine, padded, coarse


def solution(mesh):
    in_specs = (
        P(None, AXES),
        P(AXES),
        P(AXES),
        P(AXES),
        P(AXES, None, None),
        P(AXES, None, None),
    )
    out_specs = (P(None, AXES), P(None, AXES), P(None, AXES))
    return jax.shard_map(body, mesh=mesh, in_specs=in_specs, out_specs=out_specs, check_vma=False)
```

```python
import jax
import jax.numpy as jnp
from jax import lax
from jax.experimental import pallas as pl
from jax.experimental.pallas import tpu as pltpu
from jax.sharding import PartitionSpec as P

PAD = 128
AGG_DEV = 64
MODES = 6
ROWS = 4608
CHUNKS = 36
LANES = 18
PEERS = 256
AXES = ("dom", "slab")


def row_iota(shape, dtype=jnp.int32):
    return lax.broadcasted_iota(jnp.int32, shape, 0).astype(dtype)


def one_hot_rows(values_row, iota_rows, scaled=None):
    hit = iota_rows == values_row
    payload = jnp.ones_like(iota_rows) if scaled is None else scaled
    return jnp.where(hit, payload, jnp.zeros_like(iota_rows))


def as_row(value):
    return value.astype(jnp.float32).astype(jnp.bfloat16)


def nt_dot(left, right):
    return lax.dot_general(left, right, (((1,), (1,)), ((), ())), preferred_element_type=jnp.float32)


def split3(value):
    top = value.astype(jnp.bfloat16)
    rest = value - top.astype(jnp.float32)
    mid = rest.astype(jnp.bfloat16)
    low = (rest - mid.astype(jnp.float32)).astype(jnp.bfloat16)
    return top, mid, low


def pick_kernel(rows_hbm, sent_hbm, send_ref, rows_ref, sent_ref, left_ref, message_ref, arrived):
    sent_copy = pltpu.make_async_copy(sent_hbm, sent_ref, arrived.at[0])
    rows_copy = pltpu.make_async_copy(rows_hbm, rows_ref, arrived.at[1])
    sent_copy.start()
    rows_copy.start()
    rows_copy.wait()
    pad = jnp.zeros((2, 128), jnp.float32)
    for hi in range(0, 18, 2):
        for side in range(2):
            t = 2 * hi + side
            first = rows_ref[:, t * 128 : (t + 1) * 128]
            second = rows_ref[:, (t + 2) * 128 : (t + 3) * 128]
            pair = jnp.concatenate([first, pad, second, pad], axis=0)
            for s, piece in enumerate(split3(pair)):
                left_ref[hi * 8 : hi * 8 + 16, s * 256 + side * 128 : s * 256 + side * 128 + 128] = piece
    sent_copy.wait()
    lane_iota = row_iota((256, 128)).astype(jnp.float32).astype(jnp.bfloat16)
    for h in range(2):
        message_ref[...] = jnp.zeros((128, 128), jnp.float32)
        for k0 in range(0, LANES, 2):
            index = [sent_ref[k, :, h * 128 : (h + 1) * 128] for k in range(k0, k0 + 2)]
            hot = jnp.concatenate([one_hot_rows(as_row(v & 255), lane_iota) for v in index], axis=1)
            found = jnp.dot(left_ref[...], jnp.concatenate([hot] * 3, axis=0), preferred_element_type=jnp.float32)
            for n, v in enumerate(index):
                tile = jnp.broadcast_to(v >> 8, (8, 128))
                total = jnp.zeros((8, 128), jnp.float32)
                for t in range(18):
                    total = jnp.where(tile == t, found[t * 8 : t * 8 + 8, n * 128 : (n + 1) * 128], total)
                k = k0 + n
                message_ref[MODES * k : MODES * (k + 1), :] = total[0:MODES]
        send_ref[h * 128 : (h + 1) * 128, :] = message_ref[...].T


def gram_part(rows8_ref, hot_ref, left_ref):
    for c in range(CHUNKS):
        cols = slice(c * 128, (c + 1) * 128)
        x = rows8_ref[:, cols]
        for i in range(0, MODES, 2):
            one = jnp.broadcast_to(rows8_ref[i : i + 1, cols], (8, 128))
            two = jnp.broadcast_to(rows8_ref[i + 1 : i + 2, cols], (8, 128))
            pieces = split3(jnp.concatenate([x * one, x * two], axis=0))
            for s in range(3):
                left_ref[s * 48 + i * 8 : s * 48 + i * 8 + 16, cols] = pieces[s]
    full = nt_dot(left_ref[...], hot_ref[...])
    return full[0:48] + (full[48:96] + full[96:144])


def hot_aggregates(agg_row, c, hot_ref):
    iota = row_iota((AGG_DEV, 128)).astype(jnp.float32).astype(jnp.bfloat16)
    hot_ref[:, c * 128 : (c + 1) * 128] = one_hot_rows(as_row(agg_row), iota)


def of_chunk(table_ref, c):
    return table_ref[c // 2, :, (c % 2) * 128 : (c % 2) * 128 + 128]


def own_kernel(me_ref, rows_ref, owner_ref, local_ref, arrive_ref, sent_ref, gram_ref, agg_ref, hot_ref, landed_ref,
               rows8_ref, left_ref):
    owned = owner_ref[...] == me_ref[0]
    agg_ref[...] = jnp.where(owned, local_ref[...], -1)
    rows8_ref[0:MODES, :] = rows_ref[...]
    rows8_ref[MODES:8, :] = jnp.zeros((2, ROWS), jnp.float32)
    for c in range(CHUNKS):
        hot_aggregates(agg_ref[c : c + 1, :], c, hot_ref)
        hot_aggregates(of_chunk(arrive_ref, c) >> 7, c, landed_ref)
    gram_ref[...] = gram_part(rows8_ref, hot_ref, left_ref)


def apply_tables(rows8_ref, hot_ref, table_ref, put):
    table = jnp.concatenate(split3(table_ref[...]), axis=1)
    step = 2
    for c0 in range(0, CHUNKS, step):
        hot = hot_ref[:, c0 * 128 : (c0 + step) * 128]
        entry = jnp.dot(table, jnp.concatenate([hot] * 3, axis=0), preferred_element_type=jnp.float32)
        for c in range(c0, c0 + step):
            cols = slice(c * 128, (c + 1) * 128)
            part = entry[:, (c - c0) * 128 : (c - c0 + 1) * 128]
            total = jnp.broadcast_to(rows8_ref[0:1, cols], (8, 128)) * part[0:8]
            for i in range(1, MODES):
                total = total + jnp.broadcast_to(rows8_ref[i : i + 1, cols], (8, 128)) * part[i * 8 : i * 8 + 8]
            put(c, total)


def low_part(target_row, c, low_ref):
    iota = row_iota((256, 128)).astype(jnp.float32).astype(jnp.bfloat16)
    low_ref[:, c * 128 : (c + 1) * 128] = one_hot_rows(as_row(target_row & 255), iota)


def high_part(tile, target_row, high_count, c, left_ref):
    top = tile.astype(jnp.bfloat16).astype(jnp.float32)
    pieces = jnp.concatenate([top, tile - top], axis=0).astype(jnp.bfloat16)
    high = jnp.broadcast_to(as_row(target_row >> 8), (16, 128))
    zero = jnp.zeros((16, 128), jnp.bfloat16)
    for hi in range(high_count):
        left_ref[hi * 16 : hi * 16 + 16, c * 128 : (c + 1) * 128] = jnp.where(high == hi, pieces, zero)


def factor_kernel(recv_ref, landed_ref, gram_ref, send_ref, coarse_ref, table_ref, answer_ref,
                  rows8_ref, left_ref, message_ref):
    rows8_ref[MODES:8, :] = jnp.zeros((2, ROWS), jnp.float32)
    for h in range(2):
        message_ref[h] = recv_ref[h * 128 : (h + 1) * 128, :].T
        for k in range(LANES):
            c = 2 * k + h
            rows8_ref[0:MODES, c * 128 : (c + 1) * 128] = message_ref[h, MODES * k : MODES * (k + 1), :]
    gram = gram_ref[...] + gram_part(rows8_ref, landed_ref, left_ref)
    g = [[gram[i * 8 + j : i * 8 + j + 1, :] for j in range(MODES)] for i in range(MODES)]
    up = [[None] * MODES for _ in range(MODES)]
    over = [None] * MODES
    zero = jnp.zeros((1, AGG_DEV), jnp.float32)
    for i in range(MODES):
        square = g[i][i]
        for k in range(i):
            square = square - up[k][i] * up[k][i]
        pivot = jnp.sqrt(square)
        up[i][i] = pivot
        over[i] = 1.0 / pivot
        for j in range(i + 1, MODES):
            rest = g[i][j]
            for k in range(i):
                rest = rest - up[k][i] * up[k][j]
            up[i][j] = rest * over[i]
    inv = [[None] * MODES for _ in range(MODES)]
    for i in range(MODES):
        inv[i][i] = over[i]
        for j in range(i + 1, MODES):
            total = inv[i][i] * up[i][j]
            for k in range(i + 1, j):
                total = total + inv[i][k] * up[k][j]
            inv[i][j] = -total * over[j]
    table_ref[...] = jnp.zeros((48, AGG_DEV), jnp.float32)
    for i in range(MODES):
        for j in range(MODES):
            coarse_ref[i * MODES + j : i * MODES + j + 1, :] = up[i][j] if j >= i else zero
            if j >= i:
                table_ref[i * 8 + j : i * 8 + j + 1, :] = inv[i][j]

    def put(c, total):
        answer_ref[:, c * 128 : (c + 1) * 128] = total
        message_ref[c % 2, MODES * (c // 2) : MODES * (c // 2 + 1), :] = total[0:MODES]

    apply_tables(rows8_ref, landed_ref, table_ref, put)
    for h in range(2):
        send_ref[h * 128 : (h + 1) * 128, :] = message_ref[h].T


def padded_kernel(rows_ref, agg_ref, place_ref, arrive_ref, table_ref, hot_ref, answer_ref, padded_ref, own_ref, left_ref, low_ref):
    def put(c, total):
        own_ref[:, c * 128 : (c + 1) * 128] = total

    apply_tables(rows_ref, hot_ref, table_ref, put)
    for c in range(CHUNKS):
        cols = slice(c * 128, (c + 1) * 128)
        agg = agg_ref[c : c + 1, :]
        slot = jnp.where(agg >= 0, agg * 128 + place_ref[c : c + 1, :], -1)
        high_part(own_ref[:, cols], slot, 32, c, left_ref)
        low_part(slot, c, low_ref)
        landing = of_chunk(arrive_ref, c)
        high_part(answer_ref[:, cols], landing, 32, CHUNKS + c, left_ref)
        low_part(landing, CHUNKS + c, low_ref)
    found = nt_dot(left_ref[...], low_ref[...])
    for a in range(AGG_DEV):
        part = found[(a // 2) * 16 : (a // 2) * 16 + 16, (a % 2) * 128 : (a % 2) * 128 + 128]
        padded_ref[:, a * 128 : (a + 1) * 128] = part[0:MODES] + part[8 : 8 + MODES]


def fine_kernel(recv_ref, sent_ref, own_ref, fine_ref, message_ref, left_ref, low_ref):
    for h in range(2):
        message_ref[h] = recv_ref[h * 128 : (h + 1) * 128, :].T
        for k in range(LANES):
            tile = jnp.concatenate([message_ref[h, MODES * k : MODES * (k + 1), :], jnp.zeros((2, 128), jnp.float32)], axis=0)
            high_part(tile, of_chunk(sent_ref, 2 * k + h), 18, 2 * k + h, left_ref)
            low_part(of_chunk(sent_ref, 2 * k + h), 2 * k + h, low_ref)
    found = nt_dot(left_ref[...], low_ref[...])
    for c in range(CHUNKS):
        cols = slice(c * 128, (c + 1) * 128)
        part = found[(c // 2) * 16 : (c // 2) * 16 + 16, (c % 2) * 128 : (c % 2) * 128 + 128]
        fine_ref[:, cols] = own_ref[0:MODES, cols] + (part[0:MODES] + part[8 : 8 + MODES])


def f32(*shape):
    return jax.ShapeDtypeStruct(shape, jnp.float32)


def i32(*shape):
    return jax.ShapeDtypeStruct(shape, jnp.int32)


def bf16(*shape):
    return jax.ShapeDtypeStruct(shape, jnp.bfloat16)


def vm(*shape):
    return pltpu.VMEM(shape, jnp.float32)


def vb(*shape):
    return pltpu.VMEM(shape, jnp.bfloat16)


def call(kernel, out_shape, scratch, *args, mib, scalar=False, place=pltpu.VMEM):
    specs = [pl.BlockSpec(memory_space=place) for _ in args]
    if scalar:
        specs[0] = pl.BlockSpec(memory_space=pltpu.SMEM)
    many = isinstance(out_shape, tuple)
    one = pl.BlockSpec(memory_space=pltpu.VMEM)
    return pl.pallas_call(
        kernel,
        out_shape=out_shape,
        in_specs=specs,
        out_specs=tuple(one for _ in out_shape) if many else one,
        scratch_shapes=scratch,
        compiler_params=pltpu.CompilerParams(vmem_limit_bytes=mib * 1024 * 1024),
        name=kernel.__name__,
    )(*args)


def exchange(message):
    return lax.all_to_all(message, AXES, 0, 0, tiled=True)


def body(nullspace, owner_device, local_aggregate, position, sent_rows, arrival_slot):
    me = (lax.axis_index("dom") * lax.axis_size("slab") + lax.axis_index("slab")).reshape(1)
    owner = owner_device.reshape(CHUNKS, 128)
    local = local_aggregate.reshape(CHUNKS, 128)
    place = position.reshape(CHUNKS, 128)
    sent = jnp.transpose(sent_rows, (2, 0, 1))
    arrive = jnp.transpose(arrival_slot, (2, 0, 1))
    send = call(
        pick_kernel,
        f32(PEERS, 128),
        [vm(MODES, ROWS), pltpu.VMEM((LANES, 1, PEERS), jnp.int32), vb(144, 768), vm(128, 128), pltpu.SemaphoreType.DMA((2,))],
        pltpu.with_memory_space_constraint(nullspace, pltpu.HBM), pltpu.with_memory_space_constraint(sent, pltpu.HBM),
        mib=4, place=pltpu.HBM,
    )
    recv = exchange(send)
    gram, agg, hot, landed = call(
        own_kernel,
        (f32(48, AGG_DEV), i32(CHUNKS, 128), bf16(AGG_DEV, ROWS), bf16(AGG_DEV, ROWS)),
        [vm(8, ROWS), vb(144, ROWS)],
        me, nullspace, owner, local, arrive, sent,
        mib=6, scalar=True,
    )
    send, coarse, table, answer = call(
        factor_kernel,
        (f32(PEERS, 128), f32(36, AGG_DEV), f32(48, AGG_DEV), f32(8, ROWS)),
        [vm(8, ROWS), vb(144, ROWS), vm(2, 128, 128)],
        recv, landed, gram,
        mib=6,
    )
    recv = exchange(send)
    padded, own = call(
        padded_kernel,
        (f32(MODES, AGG_DEV * PAD), f32(8, ROWS)),
        [vb(512, 2 * ROWS), vb(256, 2 * ROWS)],
        nullspace, agg, place, arrive, table, hot, answer,
        mib=20,
    )
    fine = call(
        fine_kernel,
        f32(MODES, ROWS),
        [vm(2, 128, 128), vb(288, ROWS), vb(256, ROWS)],
        recv, sent, own,
        mib=6,
    )
    return fine, padded, coarse


def solution(mesh):
    in_specs = (
        P(None, AXES),
        P(AXES),
        P(AXES),
        P(AXES),
        P(AXES, None, None),
        P(AXES, None, None),
    )
    out_specs = (P(None, AXES), P(None, AXES), P(None, AXES))
    return jax.shard_map(body, mesh=mesh, in_specs=in_specs, out_specs=out_specs, check_vma=False)
```

```python
import jax
import jax.numpy as jnp
from jax import lax
from jax.experimental import pallas as pl
from jax.experimental.pallas import tpu as pltpu
from jax.sharding import PartitionSpec as P

PAD = 128
AGG_DEV = 64
MODES = 6
ROWS = 4608
CHUNKS = 36
LANES = 18
PEERS = 256
AXES = ("dom", "slab")


def row_iota(shape, dtype=jnp.int32):
    return lax.broadcasted_iota(jnp.int32, shape, 0).astype(dtype)


def one_hot_rows(values_row, iota_rows, scaled=None):
    hit = iota_rows == values_row
    payload = jnp.ones_like(iota_rows) if scaled is None else scaled
    return jnp.where(hit, payload, jnp.zeros_like(iota_rows))


def as_row(value):
    return value.astype(jnp.float32).astype(jnp.bfloat16)


def nt_dot(left, right):
    return lax.dot_general(left, right, (((1,), (1,)), ((), ())), preferred_element_type=jnp.float32)


def split3(value):
    top = value.astype(jnp.bfloat16)
    rest = value - top.astype(jnp.float32)
    mid = rest.astype(jnp.bfloat16)
    low = (rest - mid.astype(jnp.float32)).astype(jnp.bfloat16)
    return top, mid, low


def split2(value):
    top = value.astype(jnp.bfloat16)
    return top, (value - top.astype(jnp.float32)).astype(jnp.bfloat16)


def fill_table(tile_of, left_ref):
    pad = jnp.zeros((2, 128), jnp.float32)
    for hi in range(0, 18, 2):
        for side in range(2):
            pair = jnp.concatenate([tile_of(2 * hi + side), pad, tile_of(2 * hi + side + 2), pad], axis=0)
            for s, piece in enumerate(split2(pair)):
                left_ref[hi * 8 : hi * 8 + 16, s * 256 + side * 128 : s * 256 + side * 128 + 128] = piece


def gather_chunks(index, left_ref):
    iota = row_iota((256, 128)).astype(jnp.float32).astype(jnp.bfloat16)
    hot = jnp.concatenate([one_hot_rows(as_row(v & 255), iota) for v in index], axis=1)
    found = jnp.dot(left_ref[...], jnp.concatenate([hot, hot], axis=0), preferred_element_type=jnp.float32)
    result = []
    for n, v in enumerate(index):
        tile = jnp.broadcast_to(v >> 8, (8, 128))
        total = jnp.zeros((8, 128), jnp.float32)
        for t in range(18):
            total = jnp.where(tile == t, found[t * 8 : t * 8 + 8, n * 128 : (n + 1) * 128], total)
        result.append(total)
    return result


def pick_kernel(rows_hbm, sent_hbm, send_ref, rows_ref, sent_ref, left_ref, message_ref, arrived):
    sent_copy = pltpu.make_async_copy(sent_hbm, sent_ref, arrived.at[0])
    rows_copy = pltpu.make_async_copy(rows_hbm, rows_ref, arrived.at[1])
    sent_copy.start()
    rows_copy.start()
    rows_copy.wait()
    fill_table(lambda t: rows_ref[:, t * 128 : (t + 1) * 128], left_ref)
    sent_copy.wait()
    for h in range(2):
        message_ref[h, MODES * LANES : 128, :] = jnp.zeros((128 - MODES * LANES, 128), jnp.float32)
        for k0 in range(0, LANES, 2):
            index = [sent_ref[k, :, h * 128 : (h + 1) * 128] for k in range(k0, k0 + 2)]
            for n, total in enumerate(gather_chunks(index, left_ref)):
                k = k0 + n
                message_ref[h, MODES * k : MODES * (k + 1), :] = total[0:MODES]
        send_ref[h * 128 : (h + 1) * 128, :] = message_ref[h].T


def gram_part(rows8_ref, hot_ref, left_ref):
    for c in range(CHUNKS):
        cols = slice(c * 128, (c + 1) * 128)
        x = rows8_ref[:, cols]
        for i in range(0, MODES, 2):
            one = jnp.broadcast_to(rows8_ref[i : i + 1, cols], (8, 128))
            two = jnp.broadcast_to(rows8_ref[i + 1 : i + 2, cols], (8, 128))
            pieces = split3(jnp.concatenate([x * one, x * two], axis=0))
            for s in range(3):
                left_ref[s * 48 + i * 8 : s * 48 + i * 8 + 16, cols] = pieces[s]
    full = nt_dot(left_ref[...], hot_ref[...])
    return full[0:48] + (full[48:96] + full[96:144])


def hot_aggregates(agg_row, c, hot_ref):
    iota = row_iota((AGG_DEV, 128)).astype(jnp.float32).astype(jnp.bfloat16)
    hot_ref[:, c * 128 : (c + 1) * 128] = one_hot_rows(as_row(agg_row), iota)


def of_chunk(table_ref, c):
    return table_ref[c // 2, :, (c % 2) * 128 : (c % 2) * 128 + 128]


def own_kernel(me_ref, rows_ref, owner_ref, local_ref, arrive_ref, sent_ref, gram_ref, agg_ref, hot_ref, landed_ref, source_ref,
               rows8_ref, left_ref, code_ref, low_ref):
    owned = owner_ref[...] == me_ref[0]
    agg_ref[...] = jnp.where(owned, local_ref[...], -1)
    rows8_ref[0:MODES, :] = rows_ref[...]
    rows8_ref[MODES:8, :] = jnp.zeros((2, ROWS), jnp.float32)
    lanes = jnp.broadcast_to(as_row(lax.broadcasted_iota(jnp.int32, (1, 128), 1)), (48, 128))
    high_iota = row_iota((48, 128)).astype(jnp.float32).astype(jnp.bfloat16)
    low_iota = row_iota((128, 128)).astype(jnp.float32).astype(jnp.bfloat16)
    for c in range(CHUNKS):
        cols = slice(c * 128, (c + 1) * 128)
        hot_aggregates(agg_ref[c : c + 1, :], c, hot_ref)
        hot_aggregates(of_chunk(arrive_ref, c) >> 7, c, landed_ref)
        sent = of_chunk(sent_ref, c)
        high = as_row(sent >> 7)
        code_ref[0:48, cols] = one_hot_rows(high, high_iota, jnp.full_like(high_iota, c))
        code_ref[48:96, cols] = one_hot_rows(high, high_iota, lanes)
        low_ref[:, cols] = one_hot_rows(as_row(sent & 127), low_iota)
    gram_ref[...] = gram_part(rows8_ref, hot_ref, left_ref)
    code = nt_dot(code_ref[...], low_ref[...])
    slot = (code[0:CHUNKS] * 128.0 + code[48 : 48 + CHUNKS]).astype(jnp.int32)
    source_ref[...] = jnp.where(owned, -1, slot)


def apply_tables(rows8_ref, hot_ref, table_ref, put):
    table = jnp.concatenate(split3(table_ref[...]), axis=1)
    step = 2
    for c0 in range(0, CHUNKS, step):
        hot = hot_ref[:, c0 * 128 : (c0 + step) * 128]
        entry = jnp.dot(table, jnp.concatenate([hot] * 3, axis=0), preferred_element_type=jnp.float32)
        for c in range(c0, c0 + step):
            cols = slice(c * 128, (c + 1) * 128)
            part = entry[:, (c - c0) * 128 : (c - c0 + 1) * 128]
            total = jnp.broadcast_to(rows8_ref[0:1, cols], (8, 128)) * part[0:8]
            for i in range(1, MODES):
                total = total + jnp.broadcast_to(rows8_ref[i : i + 1, cols], (8, 128)) * part[i * 8 : i * 8 + 8]
            put(c, total)


def low_part(target_row, c, low_ref):
    iota = row_iota((256, 128)).astype(jnp.float32).astype(jnp.bfloat16)
    low_ref[:, c * 128 : (c + 1) * 128] = one_hot_rows(as_row(target_row & 255), iota)


def high_part(tile, target_row, high_count, c, left_ref):
    top = tile.astype(jnp.bfloat16).astype(jnp.float32)
    pieces = jnp.concatenate([top, tile - top], axis=0).astype(jnp.bfloat16)
    high = jnp.broadcast_to(as_row(target_row >> 8), (16, 128))
    zero = jnp.zeros((16, 128), jnp.bfloat16)
    for hi in range(high_count):
        left_ref[hi * 16 : hi * 16 + 16, c * 128 : (c + 1) * 128] = jnp.where(high == hi, pieces, zero)


def factor_kernel(recv_ref, landed_ref, gram_ref, send_ref, coarse_ref, table_ref, answer_ref,
                  rows8_ref, left_ref, message_ref):
    rows8_ref[MODES:8, :] = jnp.zeros((2, ROWS), jnp.float32)
    for h in range(2):
        message_ref[h] = recv_ref[h * 128 : (h + 1) * 128, :].T
        for k in range(LANES):
            c = 2 * k + h
            rows8_ref[0:MODES, c * 128 : (c + 1) * 128] = message_ref[h, MODES * k : MODES * (k + 1), :]
    gram = gram_ref[...] + gram_part(rows8_ref, landed_ref, left_ref)
    g = [[gram[i * 8 + j : i * 8 + j + 1, :] for j in range(MODES)] for i in range(MODES)]
    up = [[None] * MODES for _ in range(MODES)]
    over = [None] * MODES
    zero = jnp.zeros((1, AGG_DEV), jnp.float32)
    for i in range(MODES):
        square = g[i][i]
        for k in range(i):
            square = square - up[k][i] * up[k][i]
        pivot = jnp.sqrt(square)
        up[i][i] = pivot
        over[i] = 1.0 / pivot
        for j in range(i + 1, MODES):
            rest = g[i][j]
            for k in range(i):
                rest = rest - up[k][i] * up[k][j]
            up[i][j] = rest * over[i]
    inv = [[None] * MODES for _ in range(MODES)]
    for i in range(MODES):
        inv[i][i] = over[i]
        for j in range(i + 1, MODES):
            total = inv[i][i] * up[i][j]
            for k in range(i + 1, j):
                total = total + inv[i][k] * up[k][j]
            inv[i][j] = -total * over[j]
    table_ref[...] = jnp.zeros((48, AGG_DEV), jnp.float32)
    for i in range(MODES):
        for j in range(MODES):
            coarse_ref[i * MODES + j : i * MODES + j + 1, :] = up[i][j] if j >= i else zero
            if j >= i:
                table_ref[i * 8 + j : i * 8 + j + 1, :] = inv[i][j]

    def put(c, total):
        answer_ref[:, c * 128 : (c + 1) * 128] = total
        message_ref[c % 2, MODES * (c // 2) : MODES * (c // 2 + 1), :] = total[0:MODES]

    apply_tables(rows8_ref, landed_ref, table_ref, put)
    for h in range(2):
        send_ref[h * 128 : (h + 1) * 128, :] = message_ref[h].T


def padded_kernel(rows_ref, agg_ref, place_ref, arrive_ref, table_ref, hot_ref, answer_ref, padded_ref, own_ref, left_ref, low_ref):
    def put(c, total):
        own_ref[:, c * 128 : (c + 1) * 128] = total

    apply_tables(rows_ref, hot_ref, table_ref, put)
    for c in range(CHUNKS):
        cols = slice(c * 128, (c + 1) * 128)
        agg = agg_ref[c : c + 1, :]
        slot = jnp.where(agg >= 0, agg * 128 + place_ref[c : c + 1, :], -1)
        high_part(own_ref[:, cols], slot, 32, c, left_ref)
        low_part(slot, c, low_ref)
        landing = of_chunk(arrive_ref, c)
        high_part(answer_ref[:, cols], landing, 32, CHUNKS + c, left_ref)
        low_part(landing, CHUNKS + c, low_ref)
    found = nt_dot(left_ref[...], low_ref[...])
    for a in range(AGG_DEV):
        part = found[(a // 2) * 16 : (a // 2) * 16 + 16, (a % 2) * 128 : (a % 2) * 128 + 128]
        padded_ref[:, a * 128 : (a + 1) * 128] = part[0:MODES] + part[8 : 8 + MODES]


def fine_kernel(recv_ref, source_ref, own_ref, fine_ref, message_ref, left_ref):
    for h in range(2):
        message_ref[h] = recv_ref[h * 128 : (h + 1) * 128, :].T
    fill_table(lambda t: message_ref[t % 2, MODES * (t // 2) : MODES * (t // 2 + 1), :], left_ref)
    for c0 in range(0, CHUNKS, 2):
        index = [source_ref[c : c + 1, :] for c in range(c0, c0 + 2)]
        for n, total in enumerate(gather_chunks(index, left_ref)):
            cols = slice((c0 + n) * 128, (c0 + n + 1) * 128)
            fine_ref[:, cols] = own_ref[0:MODES, cols] + total[0:MODES]


def f32(*shape):
    return jax.ShapeDtypeStruct(shape, jnp.float32)


def i32(*shape):
    return jax.ShapeDtypeStruct(shape, jnp.int32)


def bf16(*shape):
    return jax.ShapeDtypeStruct(shape, jnp.bfloat16)


def vm(*shape):
    return pltpu.VMEM(shape, jnp.float32)


def vb(*shape):
    return pltpu.VMEM(shape, jnp.bfloat16)


def call(kernel, out_shape, scratch, *args, mib, scalar=False, place=pltpu.VMEM):
    specs = [pl.BlockSpec(memory_space=place) for _ in args]
    if scalar:
        specs[0] = pl.BlockSpec(memory_space=pltpu.SMEM)
    many = isinstance(out_shape, tuple)
    one = pl.BlockSpec(memory_space=pltpu.VMEM)
    return pl.pallas_call(
        kernel,
        out_shape=out_shape,
        in_specs=specs,
        out_specs=tuple(one for _ in out_shape) if many else one,
        scratch_shapes=scratch,
        compiler_params=pltpu.CompilerParams(vmem_limit_bytes=mib * 1024 * 1024),
        name=kernel.__name__,
    )(*args)


def exchange(message):
    return lax.all_to_all(message, AXES, 0, 0, tiled=True)


def body(nullspace, owner_device, local_aggregate, position, sent_rows, arrival_slot):
    me = (lax.axis_index("dom") * lax.axis_size("slab") + lax.axis_index("slab")).reshape(1)
    owner = owner_device.reshape(CHUNKS, 128)
    local = local_aggregate.reshape(CHUNKS, 128)
    place = position.reshape(CHUNKS, 128)
    sent = jnp.transpose(sent_rows, (2, 0, 1))
    arrive = jnp.transpose(arrival_slot, (2, 0, 1))
    send = call(
        pick_kernel,
        f32(PEERS, 128),
        [vm(MODES, ROWS), pltpu.VMEM((LANES, 1, PEERS), jnp.int32), vb(144, 512), vm(2, 128, 128), pltpu.SemaphoreType.DMA((2,))],
        pltpu.with_memory_space_constraint(nullspace, pltpu.HBM), pltpu.with_memory_space_constraint(sent, pltpu.HBM),
        mib=4, place=pltpu.HBM,
    )
    recv = exchange(send)
    gram, agg, hot, landed, source = call(
        own_kernel,
        (f32(48, AGG_DEV), i32(CHUNKS, 128), bf16(AGG_DEV, ROWS), bf16(AGG_DEV, ROWS), i32(CHUNKS, 128)),
        [vm(8, ROWS), vb(144, ROWS), vb(96, ROWS), vb(128, ROWS)],
        me, nullspace, owner, local, arrive, sent,
        mib=10, scalar=True,
    )
    send, coarse, table, answer = call(
        factor_kernel,
        (f32(PEERS, 128), f32(36, AGG_DEV), f32(48, AGG_DEV), f32(8, ROWS)),
        [vm(8, ROWS), vb(144, ROWS), vm(2, 128, 128)],
        recv, landed, gram,
        mib=6,
    )
    recv = exchange(send)
    padded, own = call(
        padded_kernel,
        (f32(MODES, AGG_DEV * PAD), f32(8, ROWS)),
        [vb(512, 2 * ROWS), vb(256, 2 * ROWS)],
        nullspace, agg, place, arrive, table, hot, answer,
        mib=20,
    )
    fine = call(
        fine_kernel,
        f32(MODES, ROWS),
        [vm(2, 128, 128), vb(144, 512)],
        recv, source, own,
        mib=6,
    )
    return fine, padded, coarse


def solution(mesh):
    in_specs = (
        P(None, AXES),
        P(AXES),
        P(AXES),
        P(AXES),
        P(AXES, None, None),
        P(AXES, None, None),
    )
    out_specs = (P(None, AXES), P(None, AXES), P(None, AXES))
    return jax.shard_map(body, mesh=mesh, in_specs=in_specs, out_specs=out_specs, check_vma=False)
```

```python
import jax
import jax.numpy as jnp
from jax import lax
from jax.experimental import pallas as pl
from jax.experimental.pallas import tpu as pltpu
from jax.sharding import PartitionSpec as P

PAD = 128
AGG_DEV = 64
MODES = 6
ROWS = 4608
CHUNKS = 36
LANES = 18
PEERS = 256
AXES = ("dom", "slab")


def row_iota(shape, dtype=jnp.int32):
    return lax.broadcasted_iota(jnp.int32, shape, 0).astype(dtype)


def one_hot_rows(values_row, iota_rows, scaled=None):
    hit = iota_rows == values_row
    payload = jnp.ones_like(iota_rows) if scaled is None else scaled
    return jnp.where(hit, payload, jnp.zeros_like(iota_rows))


def as_row(value):
    return value.astype(jnp.float32).astype(jnp.bfloat16)


def nt_dot(left, right):
    return lax.dot_general(left, right, (((1,), (1,)), ((), ())), preferred_element_type=jnp.float32)


def split3(value):
    top = value.astype(jnp.bfloat16)
    rest = value - top.astype(jnp.float32)
    mid = rest.astype(jnp.bfloat16)
    low = (rest - mid.astype(jnp.float32)).astype(jnp.bfloat16)
    return top, mid, low


def split2(value):
    top = value.astype(jnp.bfloat16)
    return top, (value - top.astype(jnp.float32)).astype(jnp.bfloat16)


def fill_table(tile_of, left_ref):
    pad = jnp.zeros((2, 128), jnp.float32)
    for hi in range(0, 18, 2):
        for side in range(2):
            pair = jnp.concatenate([tile_of(2 * hi + side), pad, tile_of(2 * hi + side + 2), pad], axis=0)
            for s, piece in enumerate(split2(pair)):
                left_ref[hi * 8 : hi * 8 + 16, s * 256 + side * 128 : s * 256 + side * 128 + 128] = piece


def gather_chunks(index, left_ref):
    iota = row_iota((256, 128)).astype(jnp.float32).astype(jnp.bfloat16)
    hot = jnp.concatenate([one_hot_rows(as_row(v & 255), iota) for v in index], axis=1)
    found = jnp.dot(left_ref[...], jnp.concatenate([hot, hot], axis=0), preferred_element_type=jnp.float32)
    result = []
    for n, v in enumerate(index):
        tile = jnp.broadcast_to(v >> 8, (8, 128))
        total = jnp.zeros((8, 128), jnp.float32)
        for t in range(18):
            total = jnp.where(tile == t, found[t * 8 : t * 8 + 8, n * 128 : (n + 1) * 128], total)
        result.append(total)
    return result


def pick_kernel(rows_hbm, sent_hbm, send_ref, rows_ref, sent_ref, left_ref, message_ref, arrived):
    sent_copy = pltpu.make_async_copy(sent_hbm, sent_ref, arrived.at[0])
    rows_copy = pltpu.make_async_copy(rows_hbm, rows_ref, arrived.at[1])
    sent_copy.start()
    rows_copy.start()
    rows_copy.wait()
    fill_table(lambda t: rows_ref[:, t * 128 : (t + 1) * 128], left_ref)
    sent_copy.wait()
    for h in range(2):
        message_ref[h, MODES * LANES : 128, :] = jnp.zeros((128 - MODES * LANES, 128), jnp.float32)
        for k0 in range(0, LANES, 2):
            index = [sent_ref[k, :, h * 128 : (h + 1) * 128] for k in range(k0, k0 + 2)]
            for n, total in enumerate(gather_chunks(index, left_ref)):
                k = k0 + n
                message_ref[h, MODES * k : MODES * (k + 1), :] = total[0:MODES]
        send_ref[h * 128 : (h + 1) * 128, :] = message_ref[h].T


def gram_part(rows_ref, hot_ref, left_ref):
    for c in range(CHUNKS):
        cols = slice(c * 128, (c + 1) * 128)
        x = rows_ref[0:8, cols]
        for d in range(0, 4, 2):
            pieces = split3(jnp.concatenate([x * rows_ref[d : d + 8, cols], x * rows_ref[d + 1 : d + 9, cols]], axis=0))
            for s in range(3):
                left_ref[s * 32 + d * 8 : s * 32 + d * 8 + 16, cols] = pieces[s]
    full = nt_dot(left_ref[...], hot_ref[...])
    return full[0:32] + (full[32:64] + full[64:96])


def gram_row(i, j):
    d = (j - i) % MODES
    return 8 * d + i if d <= 3 else 8 * (MODES - d) + j


def hot_aggregates(agg_row, c, hot_ref):
    iota = row_iota((AGG_DEV, 128)).astype(jnp.float32).astype(jnp.bfloat16)
    hot_ref[:, c * 128 : (c + 1) * 128] = one_hot_rows(as_row(agg_row), iota)


def of_chunk(table_ref, c):
    return table_ref[c // 2, :, (c % 2) * 128 : (c % 2) * 128 + 128]


def own_kernel(me_ref, rows_ref, owner_ref, local_ref, arrive_ref, sent_ref, gram_ref, agg_ref, hot_ref, landed_ref, source_ref,
               twice_ref, left_ref, code_ref, low_ref):
    owned = owner_ref[...] == me_ref[0]
    agg_ref[...] = jnp.where(owned, local_ref[...], -1)
    twice_ref[0:MODES, :] = rows_ref[...]
    twice_ref[MODES : 2 * MODES, :] = rows_ref[...]
    lanes = jnp.broadcast_to(as_row(lax.broadcasted_iota(jnp.int32, (1, 128), 1)), (48, 128))
    high_iota = row_iota((48, 128)).astype(jnp.float32).astype(jnp.bfloat16)
    low_iota = row_iota((128, 128)).astype(jnp.float32).astype(jnp.bfloat16)
    for c in range(CHUNKS):
        cols = slice(c * 128, (c + 1) * 128)
        hot_aggregates(agg_ref[c : c + 1, :], c, hot_ref)
        hot_aggregates(of_chunk(arrive_ref, c) >> 7, c, landed_ref)
        sent = of_chunk(sent_ref, c)
        high = as_row(sent >> 7)
        code_ref[0:48, cols] = one_hot_rows(high, high_iota, jnp.full_like(high_iota, c))
        code_ref[48:96, cols] = one_hot_rows(high, high_iota, lanes)
        low_ref[:, cols] = one_hot_rows(as_row(sent & 127), low_iota)
    gram_ref[...] = gram_part(twice_ref, hot_ref, left_ref)
    code = nt_dot(code_ref[...], low_ref[...])
    slot = (code[0:CHUNKS] * 128.0 + code[48 : 48 + CHUNKS]).astype(jnp.int32)
    source_ref[...] = jnp.where(owned, -1, slot)


def apply_tables(rows_ref, hot_ref, table_ref, put):
    table = jnp.concatenate(split3(table_ref[...]), axis=1)
    step = 2
    for c0 in range(0, CHUNKS, step):
        hot = hot_ref[:, c0 * 128 : (c0 + step) * 128]
        entry = jnp.dot(table, jnp.concatenate([hot] * 3, axis=0), preferred_element_type=jnp.float32)
        for c in range(c0, c0 + step):
            cols = slice(c * 128, (c + 1) * 128)
            part = entry[:, (c - c0) * 128 : (c - c0 + 1) * 128]
            total = jnp.broadcast_to(rows_ref[0:1, cols], (8, 128)) * part[0:8]
            for i in range(1, MODES):
                total = total + jnp.broadcast_to(rows_ref[i : i + 1, cols], (8, 128)) * part[i * 8 : i * 8 + 8]
            put(c, total)


def low_part(target_row, c, low_ref):
    iota = row_iota((256, 128)).astype(jnp.float32).astype(jnp.bfloat16)
    low_ref[:, c * 128 : (c + 1) * 128] = one_hot_rows(as_row(target_row & 255), iota)


def high_part(tile, target_row, high_count, c, left_ref):
    top = tile.astype(jnp.bfloat16).astype(jnp.float32)
    pieces = jnp.concatenate([top, tile - top], axis=0).astype(jnp.bfloat16)
    high = jnp.broadcast_to(as_row(target_row >> 8), (16, 128))
    zero = jnp.zeros((16, 128), jnp.bfloat16)
    for hi in range(high_count):
        left_ref[hi * 16 : hi * 16 + 16, c * 128 : (c + 1) * 128] = jnp.where(high == hi, pieces, zero)


def factor_kernel(recv_ref, landed_ref, gram_ref, send_ref, coarse_ref, table_ref, answer_ref,
                  twice_ref, left_ref, message_ref):
    for h in range(2):
        message_ref[h] = recv_ref[h * 128 : (h + 1) * 128, :].T
        for k in range(LANES):
            c = 2 * k + h
            tile = message_ref[h, MODES * k : MODES * (k + 1), :]
            twice_ref[0:MODES, c * 128 : (c + 1) * 128] = tile
            twice_ref[MODES : 2 * MODES, c * 128 : (c + 1) * 128] = tile
    gram = gram_ref[...] + gram_part(twice_ref, landed_ref, left_ref)
    g = [[gram[gram_row(i, j) : gram_row(i, j) + 1, :] for j in range(MODES)] for i in range(MODES)]
    up = [[None] * MODES for _ in range(MODES)]
    over = [None] * MODES
    zero = jnp.zeros((1, AGG_DEV), jnp.float32)
    for i in range(MODES):
        square = g[i][i]
        for k in range(i):
            square = square - up[k][i] * up[k][i]
        pivot = jnp.sqrt(square)
        up[i][i] = pivot
        over[i] = 1.0 / pivot
        for j in range(i + 1, MODES):
            rest = g[i][j]
            for k in range(i):
                rest = rest - up[k][i] * up[k][j]
            up[i][j] = rest * over[i]
    inv = [[None] * MODES for _ in range(MODES)]
    for i in range(MODES):
        inv[i][i] = over[i]
        for j in range(i + 1, MODES):
            total = inv[i][i] * up[i][j]
            for k in range(i + 1, j):
                total = total + inv[i][k] * up[k][j]
            inv[i][j] = -total * over[j]
    table_ref[...] = jnp.zeros((48, AGG_DEV), jnp.float32)
    for i in range(MODES):
        for j in range(MODES):
            coarse_ref[i * MODES + j : i * MODES + j + 1, :] = up[i][j] if j >= i else zero
            if j >= i:
                table_ref[i * 8 + j : i * 8 + j + 1, :] = inv[i][j]

    def put(c, total):
        answer_ref[:, c * 128 : (c + 1) * 128] = total
        message_ref[c % 2, MODES * (c // 2) : MODES * (c // 2 + 1), :] = total[0:MODES]

    apply_tables(twice_ref, landed_ref, table_ref, put)
    for h in range(2):
        send_ref[h * 128 : (h + 1) * 128, :] = message_ref[h].T


def padded_kernel(rows_ref, agg_ref, place_ref, arrive_ref, table_ref, hot_ref, answer_ref, padded_ref, own_ref, left_ref, low_ref):
    def put(c, total):
        own_ref[:, c * 128 : (c + 1) * 128] = total

    apply_tables(rows_ref, hot_ref, table_ref, put)
    for c in range(CHUNKS):
        cols = slice(c * 128, (c + 1) * 128)
        agg = agg_ref[c : c + 1, :]
        slot = jnp.where(agg >= 0, agg * 128 + place_ref[c : c + 1, :], -1)
        high_part(own_ref[:, cols], slot, 32, c, left_ref)
        low_part(slot, c, low_ref)
        landing = of_chunk(arrive_ref, c)
        high_part(answer_ref[:, cols], landing, 32, CHUNKS + c, left_ref)
        low_part(landing, CHUNKS + c, low_ref)
    found = nt_dot(left_ref[...], low_ref[...])
    for a in range(AGG_DEV):
        part = found[(a // 2) * 16 : (a // 2) * 16 + 16, (a % 2) * 128 : (a % 2) * 128 + 128]
        padded_ref[:, a * 128 : (a + 1) * 128] = part[0:MODES] + part[8 : 8 + MODES]


def fine_kernel(recv_ref, source_ref, own_ref, fine_ref, message_ref, left_ref):
    for h in range(2):
        message_ref[h] = recv_ref[h * 128 : (h + 1) * 128, :].T
    fill_table(lambda t: message_ref[t % 2, MODES * (t // 2) : MODES * (t // 2 + 1), :], left_ref)
    for c0 in range(0, CHUNKS, 2):
        index = [source_ref[c : c + 1, :] for c in range(c0, c0 + 2)]
        for n, total in enumerate(gather_chunks(index, left_ref)):
            cols = slice((c0 + n) * 128, (c0 + n + 1) * 128)
            fine_ref[:, cols] = own_ref[0:MODES, cols] + total[0:MODES]


def f32(*shape):
    return jax.ShapeDtypeStruct(shape, jnp.float32)


def i32(*shape):
    return jax.ShapeDtypeStruct(shape, jnp.int32)


def bf16(*shape):
    return jax.ShapeDtypeStruct(shape, jnp.bfloat16)


def vm(*shape):
    return pltpu.VMEM(shape, jnp.float32)


def vb(*shape):
    return pltpu.VMEM(shape, jnp.bfloat16)


def call(kernel, out_shape, scratch, *args, mib, scalar=False, place=pltpu.VMEM):
    specs = [pl.BlockSpec(memory_space=place) for _ in args]
    if scalar:
        specs[0] = pl.BlockSpec(memory_space=pltpu.SMEM)
    many = isinstance(out_shape, tuple)
    one = pl.BlockSpec(memory_space=pltpu.VMEM)
    return pl.pallas_call(
        kernel,
        out_shape=out_shape,
        in_specs=specs,
        out_specs=tuple(one for _ in out_shape) if many else one,
        scratch_shapes=scratch,
        compiler_params=pltpu.CompilerParams(vmem_limit_bytes=mib * 1024 * 1024),
        name=kernel.__name__,
    )(*args)


def exchange(message):
    return lax.all_to_all(message, AXES, 0, 0, tiled=True)


def body(nullspace, owner_device, local_aggregate, position, sent_rows, arrival_slot):
    me = (lax.axis_index("dom") * lax.axis_size("slab") + lax.axis_index("slab")).reshape(1)
    owner = owner_device.reshape(CHUNKS, 128)
    local = local_aggregate.reshape(CHUNKS, 128)
    place = position.reshape(CHUNKS, 128)
    sent = jnp.transpose(sent_rows, (2, 0, 1))
    arrive = jnp.transpose(arrival_slot, (2, 0, 1))
    send = call(
        pick_kernel,
        f32(PEERS, 128),
        [vm(MODES, ROWS), pltpu.VMEM((LANES, 1, PEERS), jnp.int32), vb(144, 512), vm(2, 128, 128), pltpu.SemaphoreType.DMA((2,))],
        pltpu.with_memory_space_constraint(nullspace, pltpu.HBM), pltpu.with_memory_space_constraint(sent, pltpu.HBM),
        mib=4, place=pltpu.HBM,
    )
    recv = exchange(send)
    gram, agg, hot, landed, source = call(
        own_kernel,
        (f32(32, AGG_DEV), i32(CHUNKS, 128), bf16(AGG_DEV, ROWS), bf16(AGG_DEV, ROWS), i32(CHUNKS, 128)),
        [vm(12, ROWS), vb(96, ROWS), vb(96, ROWS), vb(128, ROWS)],
        me, nullspace, owner, local, arrive, sent,
        mib=10, scalar=True,
    )
    send, coarse, table, answer = call(
        factor_kernel,
        (f32(PEERS, 128), f32(36, AGG_DEV), f32(48, AGG_DEV), f32(8, ROWS)),
        [vm(12, ROWS), vb(96, ROWS), vm(2, 128, 128)],
        recv, landed, gram,
        mib=6,
    )
    recv = exchange(send)
    padded, own = call(
        padded_kernel,
        (f32(MODES, AGG_DEV * PAD), f32(8, ROWS)),
        [vb(512, 2 * ROWS), vb(256, 2 * ROWS)],
        nullspace, agg, place, arrive, table, hot, answer,
        mib=20,
    )
    fine = call(
        fine_kernel,
        f32(MODES, ROWS),
        [vm(2, 128, 128), vb(144, 512)],
        recv, source, own,
        mib=6,
    )
    return fine, padded, coarse


def solution(mesh):
    in_specs = (
        P(None, AXES),
        P(AXES),
        P(AXES),
        P(AXES),
        P(AXES, None, None),
        P(AXES, None, None),
    )
    out_specs = (P(None, AXES), P(None, AXES), P(None, AXES))
    return jax.shard_map(body, mesh=mesh, in_specs=in_specs, out_specs=out_specs, check_vma=False)
```

```python
import jax
import jax.numpy as jnp
from jax import lax
from jax.experimental import pallas as pl
from jax.experimental.pallas import tpu as pltpu
from jax.sharding import PartitionSpec as P

PAD = 128
AGG_DEV = 64
MODES = 6
ROWS = 4608
CHUNKS = 36
LANES = 18
PEERS = 256
AXES = ("dom", "slab")


def row_iota(shape, dtype=jnp.int32):
    return lax.broadcasted_iota(jnp.int32, shape, 0).astype(dtype)


def one_hot_rows(values_row, iota_rows, scaled=None):
    hit = iota_rows == values_row
    payload = jnp.ones_like(iota_rows) if scaled is None else scaled
    return jnp.where(hit, payload, jnp.zeros_like(iota_rows))


def as_row(value):
    return value.astype(jnp.float32).astype(jnp.bfloat16)


def nt_dot(left, right):
    return lax.dot_general(left, right, (((1,), (1,)), ((), ())), preferred_element_type=jnp.float32)


def split3(value):
    top = value.astype(jnp.bfloat16)
    rest = value - top.astype(jnp.float32)
    mid = rest.astype(jnp.bfloat16)
    low = (rest - mid.astype(jnp.float32)).astype(jnp.bfloat16)
    return top, mid, low


def split2(value):
    top = value.astype(jnp.bfloat16)
    return top, (value - top.astype(jnp.float32)).astype(jnp.bfloat16)


def fill_table(tile_of, left_ref):
    pad = jnp.zeros((2, 128), jnp.float32)
    for hi in range(0, 18, 2):
        for side in range(2):
            pair = jnp.concatenate([tile_of(2 * hi + side), pad, tile_of(2 * hi + side + 2), pad], axis=0)
            for s, piece in enumerate(split2(pair)):
                left_ref[hi * 8 : hi * 8 + 16, s * 256 + side * 128 : s * 256 + side * 128 + 128] = piece


def gather_chunks(index, left_ref):
    iota = row_iota((256, 128)).astype(jnp.float32).astype(jnp.bfloat16)
    hot = jnp.concatenate([one_hot_rows(as_row(v & 255), iota) for v in index], axis=1)
    found = jnp.dot(left_ref[...], jnp.concatenate([hot, hot], axis=0), preferred_element_type=jnp.float32)
    result = []
    for n, v in enumerate(index):
        tile = jnp.broadcast_to(v >> 8, (8, 128))
        total = jnp.zeros((8, 128), jnp.float32)
        for t in range(18):
            total = jnp.where(tile == t, found[t * 8 : t * 8 + 8, n * 128 : (n + 1) * 128], total)
        result.append(total)
    return result


def pick_kernel(rows_hbm, sent_hbm, send_ref, rows_ref, sent_ref, left_ref, message_ref, arrived):
    sent_copy = pltpu.make_async_copy(sent_hbm, sent_ref, arrived.at[0])
    parts = [pl.ds(n * 1152, 1152) for n in range(4)]
    rows_copies = [pltpu.make_async_copy(rows_hbm.at[:, part], rows_ref.at[:, part], arrived.at[1 + n]) for n, part in enumerate(parts)]
    sent_copy.start()
    for copy in rows_copies:
        copy.start()
    for copy in rows_copies:
        copy.wait()
    fill_table(lambda t: rows_ref[:, t * 128 : (t + 1) * 128], left_ref)
    sent_copy.wait()
    for h in range(2):
        message_ref[h, MODES * LANES : 128, :] = jnp.zeros((128 - MODES * LANES, 128), jnp.float32)
        for k0 in range(0, LANES, 2):
            index = [sent_ref[k, :, h * 128 : (h + 1) * 128] for k in range(k0, k0 + 2)]
            for n, total in enumerate(gather_chunks(index, left_ref)):
                k = k0 + n
                message_ref[h, MODES * k : MODES * (k + 1), :] = total[0:MODES]
        send_ref[h * 128 : (h + 1) * 128, :] = message_ref[h].T


def gram_part(rows_ref, hot_ref, left_ref):
    for c in range(CHUNKS):
        cols = slice(c * 128, (c + 1) * 128)
        x = rows_ref[0:8, cols]
        for d in range(0, 4, 2):
            pieces = split3(jnp.concatenate([x * rows_ref[d : d + 8, cols], x * rows_ref[d + 1 : d + 9, cols]], axis=0))
            for s in range(3):
                left_ref[s * 32 + d * 8 : s * 32 + d * 8 + 16, cols] = pieces[s]
    full = nt_dot(left_ref[...], hot_ref[...])
    return full[0:32] + (full[32:64] + full[64:96])


def gram_row(i, j):
    d = (j - i) % MODES
    return 8 * d + i if d <= 3 else 8 * (MODES - d) + j


def hot_aggregates(agg_row, c, hot_ref):
    iota = row_iota((AGG_DEV, 128)).astype(jnp.float32).astype(jnp.bfloat16)
    hot_ref[:, c * 128 : (c + 1) * 128] = one_hot_rows(as_row(agg_row), iota)


def of_chunk(table_ref, c):
    return table_ref[c // 2, :, (c % 2) * 128 : (c % 2) * 128 + 128]


def own_kernel(me_ref, rows_ref, owner_ref, local_ref, arrive_ref, sent_ref, gram_ref, agg_ref, hot_ref, landed_ref, source_ref,
               twice_ref, left_ref, code_ref, low_ref):
    owned = owner_ref[...] == me_ref[0]
    agg_ref[...] = jnp.where(owned, local_ref[...], -1)
    twice_ref[0:MODES, :] = rows_ref[...]
    twice_ref[MODES : 2 * MODES, :] = rows_ref[...]
    lanes = jnp.broadcast_to(as_row(lax.broadcasted_iota(jnp.int32, (1, 128), 1)), (48, 128))
    high_iota = row_iota((48, 128)).astype(jnp.float32).astype(jnp.bfloat16)
    low_iota = row_iota((128, 128)).astype(jnp.float32).astype(jnp.bfloat16)
    for c in range(CHUNKS):
        cols = slice(c * 128, (c + 1) * 128)
        hot_aggregates(agg_ref[c : c + 1, :], c, hot_ref)
        hot_aggregates(of_chunk(arrive_ref, c) >> 7, c, landed_ref)
        sent = of_chunk(sent_ref, c)
        high = as_row(sent >> 7)
        code_ref[0:48, cols] = one_hot_rows(high, high_iota, jnp.full_like(high_iota, c))
        code_ref[48:96, cols] = one_hot_rows(high, high_iota, lanes)
        low_ref[:, cols] = one_hot_rows(as_row(sent & 127), low_iota)
    gram_ref[...] = gram_part(twice_ref, hot_ref, left_ref)
    code = nt_dot(code_ref[...], low_ref[...])
    slot = (code[0:CHUNKS] * 128.0 + code[48 : 48 + CHUNKS]).astype(jnp.int32)
    source_ref[...] = jnp.where(owned, -1, slot)


def apply_tables(rows_ref, hot_ref, table_ref, put):
    table = jnp.concatenate(split3(table_ref[...]), axis=1)
    step = 6
    for c0 in range(0, CHUNKS, step):
        hot = hot_ref[:, c0 * 128 : (c0 + step) * 128]
        entry = jnp.dot(table, jnp.concatenate([hot] * 3, axis=0), preferred_element_type=jnp.float32)
        for c in range(c0, c0 + step):
            cols = slice(c * 128, (c + 1) * 128)
            part = entry[:, (c - c0) * 128 : (c - c0 + 1) * 128]
            total = jnp.broadcast_to(rows_ref[0:1, cols], (8, 128)) * part[0:8]
            for i in range(1, MODES):
                total = total + jnp.broadcast_to(rows_ref[i : i + 1, cols], (8, 128)) * part[i * 8 : i * 8 + 8]
            put(c, total)


def low_part(target_row, c, low_ref):
    iota = row_iota((256, 128)).astype(jnp.float32).astype(jnp.bfloat16)
    low_ref[:, c * 128 : (c + 1) * 128] = one_hot_rows(as_row(target_row & 255), iota)


def high_part(tile, target_row, high_count, c, left_ref):
    top = tile.astype(jnp.bfloat16).astype(jnp.float32)
    pieces = jnp.concatenate([top, tile - top], axis=0).astype(jnp.bfloat16)
    high = jnp.broadcast_to(as_row(target_row >> 8), (16, 128))
    zero = jnp.zeros((16, 128), jnp.bfloat16)
    for hi in range(high_count):
        left_ref[hi * 16 : hi * 16 + 16, c * 128 : (c + 1) * 128] = jnp.where(high == hi, pieces, zero)


def factor_kernel(recv_ref, landed_ref, gram_ref, send_ref, coarse_ref, table_ref, answer_ref,
                  twice_ref, left_ref, message_ref):
    for h in range(2):
        message_ref[h] = recv_ref[h * 128 : (h + 1) * 128, :].T
        for k in range(LANES):
            c = 2 * k + h
            tile = message_ref[h, MODES * k : MODES * (k + 1), :]
            twice_ref[0:MODES, c * 128 : (c + 1) * 128] = tile
            twice_ref[MODES : 2 * MODES, c * 128 : (c + 1) * 128] = tile
    gram = gram_ref[...] + gram_part(twice_ref, landed_ref, left_ref)
    g = [[gram[gram_row(i, j) : gram_row(i, j) + 1, :] for j in range(MODES)] for i in range(MODES)]
    up = [[None] * MODES for _ in range(MODES)]
    over = [None] * MODES
    zero = jnp.zeros((1, AGG_DEV), jnp.float32)
    for i in range(MODES):
        square = g[i][i]
        for k in range(i):
            square = square - up[k][i] * up[k][i]
        pivot = jnp.sqrt(square)
        up[i][i] = pivot
        over[i] = 1.0 / pivot
        for j in range(i + 1, MODES):
            rest = g[i][j]
            for k in range(i):
                rest = rest - up[k][i] * up[k][j]
            up[i][j] = rest * over[i]
    inv = [[None] * MODES for _ in range(MODES)]
    for i in range(MODES):
        inv[i][i] = over[i]
        for j in range(i + 1, MODES):
            total = inv[i][i] * up[i][j]
            for k in range(i + 1, j):
                total = total + inv[i][k] * up[k][j]
            inv[i][j] = -total * over[j]
    table_ref[...] = jnp.zeros((48, AGG_DEV), jnp.float32)
    for i in range(MODES):
        for j in range(MODES):
            coarse_ref[i * MODES + j : i * MODES + j + 1, :] = up[i][j] if j >= i else zero
            if j >= i:
                table_ref[i * 8 + j : i * 8 + j + 1, :] = inv[i][j]

    def put(c, total):
        answer_ref[:, c * 128 : (c + 1) * 128] = total
        message_ref[c % 2, MODES * (c // 2) : MODES * (c // 2 + 1), :] = total[0:MODES]

    apply_tables(twice_ref, landed_ref, table_ref, put)
    for h in range(2):
        send_ref[h * 128 : (h + 1) * 128, :] = message_ref[h].T


def padded_kernel(rows_ref, agg_ref, place_ref, arrive_ref, table_ref, hot_ref, answer_ref, padded_ref, own_ref, left_ref, low_ref):
    def put(c, total):
        own_ref[:, c * 128 : (c + 1) * 128] = total

    apply_tables(rows_ref, hot_ref, table_ref, put)
    for c in range(CHUNKS):
        cols = slice(c * 128, (c + 1) * 128)
        agg = agg_ref[c : c + 1, :]
        slot = jnp.where(agg >= 0, agg * 128 + place_ref[c : c + 1, :], -1)
        high_part(own_ref[:, cols], slot, 32, c, left_ref)
        low_part(slot, c, low_ref)
        landing = of_chunk(arrive_ref, c)
        high_part(answer_ref[:, cols], landing, 32, CHUNKS + c, left_ref)
        low_part(landing, CHUNKS + c, low_ref)
    found = nt_dot(left_ref[...], low_ref[...])
    for a in range(AGG_DEV):
        part = found[(a // 2) * 16 : (a // 2) * 16 + 16, (a % 2) * 128 : (a % 2) * 128 + 128]
        padded_ref[:, a * 128 : (a + 1) * 128] = part[0:MODES] + part[8 : 8 + MODES]


def fine_kernel(recv_ref, source_ref, own_ref, fine_ref, message_ref, left_ref):
    for h in range(2):
        message_ref[h] = recv_ref[h * 128 : (h + 1) * 128, :].T
    fill_table(lambda t: message_ref[t % 2, MODES * (t // 2) : MODES * (t // 2 + 1), :], left_ref)
    for c0 in range(0, CHUNKS, 2):
        index = [source_ref[c : c + 1, :] for c in range(c0, c0 + 2)]
        for n, total in enumerate(gather_chunks(index, left_ref)):
            cols = slice((c0 + n) * 128, (c0 + n + 1) * 128)
            fine_ref[:, cols] = own_ref[0:MODES, cols] + total[0:MODES]


def f32(*shape):
    return jax.ShapeDtypeStruct(shape, jnp.float32)


def i32(*shape):
    return jax.ShapeDtypeStruct(shape, jnp.int32)


def bf16(*shape):
    return jax.ShapeDtypeStruct(shape, jnp.bfloat16)


def vm(*shape):
    return pltpu.VMEM(shape, jnp.float32)


def vb(*shape):
    return pltpu.VMEM(shape, jnp.bfloat16)


def call(kernel, out_shape, scratch, *args, mib, scalar=False, place=pltpu.VMEM):
    specs = [pl.BlockSpec(memory_space=place) for _ in args]
    if scalar:
        specs[0] = pl.BlockSpec(memory_space=pltpu.SMEM)
    many = isinstance(out_shape, tuple)
    one = pl.BlockSpec(memory_space=pltpu.VMEM)
    return pl.pallas_call(
        kernel,
        out_shape=out_shape,
        in_specs=specs,
        out_specs=tuple(one for _ in out_shape) if many else one,
        scratch_shapes=scratch,
        compiler_params=pltpu.CompilerParams(vmem_limit_bytes=mib * 1024 * 1024),
        name=kernel.__name__,
    )(*args)


def exchange(message):
    return lax.all_to_all(message, AXES, 0, 0, tiled=True)


def body(nullspace, owner_device, local_aggregate, position, sent_rows, arrival_slot):
    me = (lax.axis_index("dom") * lax.axis_size("slab") + lax.axis_index("slab")).reshape(1)
    owner = owner_device.reshape(CHUNKS, 128)
    local = local_aggregate.reshape(CHUNKS, 128)
    place = position.reshape(CHUNKS, 128)
    sent = jnp.transpose(sent_rows, (2, 0, 1))
    arrive = jnp.transpose(arrival_slot, (2, 0, 1))
    send = call(
        pick_kernel,
        f32(PEERS, 128),
        [vm(MODES, ROWS), pltpu.VMEM((LANES, 1, PEERS), jnp.int32), vb(144, 512), vm(2, 128, 128), pltpu.SemaphoreType.DMA((5,))],
        pltpu.with_memory_space_constraint(nullspace, pltpu.HBM), pltpu.with_memory_space_constraint(sent, pltpu.HBM),
        mib=4, place=pltpu.HBM,
    )
    recv = exchange(send)
    gram, agg, hot, landed, source = call(
        own_kernel,
        (f32(32, AGG_DEV), i32(CHUNKS, 128), bf16(AGG_DEV, ROWS), bf16(AGG_DEV, ROWS), i32(CHUNKS, 128)),
        [vm(12, ROWS), vb(96, ROWS), vb(96, ROWS), vb(128, ROWS)],
        me, nullspace, owner, local, arrive, sent,
        mib=10, scalar=True,
    )
    send, coarse, table, answer = call(
        factor_kernel,
        (f32(PEERS, 128), f32(36, AGG_DEV), f32(48, AGG_DEV), f32(8, ROWS)),
        [vm(12, ROWS), vb(96, ROWS), vm(2, 128, 128)],
        recv, landed, gram,
        mib=6,
    )
    recv = exchange(send)
    padded, own = call(
        padded_kernel,
        (f32(MODES, AGG_DEV * PAD), f32(8, ROWS)),
        [vb(512, 2 * ROWS), vb(256, 2 * ROWS)],
        nullspace, agg, place, arrive, table, hot, answer,
        mib=20,
    )
    fine = call(
        fine_kernel,
        f32(MODES, ROWS),
        [vm(2, 128, 128), vb(144, 512)],
        recv, source, own,
        mib=6,
    )
    return fine, padded, coarse


def solution(mesh):
    in_specs = (
        P(None, AXES),
        P(AXES),
        P(AXES),
        P(AXES),
        P(AXES, None, None),
        P(AXES, None, None),
    )
    out_specs = (P(None, AXES), P(None, AXES), P(None, AXES))
    return jax.shard_map(body, mesh=mesh, in_specs=in_specs, out_specs=out_specs, check_vma=False)
```
